256 devices in a mesh: freq: 8 (over z), tile: 32 (over y, x, core).
Axes of the slice: x: 4, y: 4, z: 8, core: 2. Of those that a mesh axis runs over, the one named last changes fastest.
Arguments:
- start_field: float32 [2, 8, 16384, 128], P(None, 'freq', 'tile'), may hold values from -6 to 6
- u_tiles: bfloat16 [2, 8, 32, 32, 64, 512], P(None, 'freq', 'tile'), may hold values from -0.09375 to 0.09375
- v_tiles: bfloat16 [2, 8, 32, 32, 64, 512], P(None, 'freq', None, 'tile'), may hold values from -0.1875 to 0.1875
- ranks: int32 [8, 32, 32], P('freq'), may hold values from 16 to 64, as said below
- onset_rec: int32 [32], P('tile'), may hold values from 8 to 24
- onset_src: int32 [32], P('tile'), may hold values from 8 to 24
Outputs:
- plus_field: float32 [2, 8, 16384, 128], P(None, 'freq', 'tile')
- minus_field: float32 [2, 8, 16384, 128], P(None, 'freq', 'tile')
The draws below stay inside these ranges and needn't reach their ends.
Inputs may be any that keep to these rules, and one draw needn't show every extreme that they name: `ranks`: every rank is 16, 32 or 64, and 64 occurs at every frequency.
All inputs are finite; a program needn't handle non-finite values.
Results may differ from the reference program's by a relative error of at most 0.0065.
Values may be sent and summed in bfloat16 or wider, within the bound.
A program may use at most 64 MiB of HBM per device.

```python
import math
import jax
import jax.numpy as jnp
from jax import lax

NP = 128
NBR = 512
NBC = 512
RMAX = 64
ITERS = 2
NTR = 32
NTC = 32
F = 8
NTIME = 32
NR = 16384
NS = 16384


def draw_ranks(key, part):
    key = jax.random.fold_in(key, 7)
    levels = jax.random.randint(key, (F, NTR, NTC), 0, 3)
    levels = levels.at[:, 0, 0].set(2)
    return jnp.where(levels == 0, 16, jnp.where(levels == 1, 32, 64)).astype(jnp.int32)


def touch_ends(values, stream_key, smallest, largest):
    extent = values.shape
    spot = [jax.random.randint(jax.random.fold_in(stream_key, axis), (), 0, extent[axis]) for axis in range(len(extent))]
    values = values.at[tuple(spot)].set(smallest)
    longest = extent.index(max(extent))
    spot[longest] = (spot[longest] + 1) % extent[longest]
    return values.at[tuple(spot)].set(largest)


def level_of(key, shape, cuts, low, top_value):
    factor_of = 1.0
    for dim, parts in cuts:
        heights = jax.random.uniform(jax.random.fold_in(jax.random.fold_in(key, 6), dim), (parts,), jnp.float32, low / len(cuts), top_value / len(cuts))
        factor_of = factor_of * jnp.repeat(jnp.exp(heights), shape[dim] // parts).reshape((-1,) + (1,) * (len(shape) - 1 - dim))
    return factor_of


def centred(key, dims, deviation, bound, cuts=(), held_as=jnp.bfloat16):
    level = level_of(key, dims, cuts, -0.22, 0.18) if cuts else 1.0
    values = jax.random.normal(key, dims, jnp.float32) * deviation * level
    return jnp.minimum(jnp.maximum(values, -bound), bound).astype(held_as)


def setup_inputs(seed: int = 0) -> dict:
    key_list = jax.random.split(jax.random.key(seed), 7)
    return {
        "start_field": centred(key_list[0], (2, F, NS, NP), 1.0, 6.0, ((1, 8), (2, 32)), jnp.float32),
        "u_tiles": centred(key_list[1], (2, F, NTR, NTC, RMAX, NBR), (2 * NTC * RMAX) ** -0.5, 0.09375, ((1, 8), (2, 32))),
        "v_tiles": centred(key_list[2], (2, F, NTR, NTC, RMAX, NBC), (2 * NBC) ** -0.5, 0.1875, ((1, 8), (3, 32))),
        "ranks": draw_ranks(jax.random.fold_in(key_list[6], 71), 0),
        "onset_rec": touch_ends(jax.random.randint(key_list[4], (NTR,), NTIME // 4, 3 * NTIME // 4 + 1), jax.random.fold_in(key_list[4], 1), NTIME // 4, (3 * NTIME // 4 + 1) - 1).astype(jnp.int32),
        "onset_src": touch_ends(jax.random.randint(key_list[5], (NTC,), NTIME // 4, 3 * NTIME // 4 + 1), jax.random.fold_in(key_list[5], 1), NTIME // 4, (3 * NTIME // 4 + 1) - 1).astype(jnp.int32),
    }


def window_matrix(onset, count_freq):
    total_time = 4 * count_freq
    times = jnp.arange(total_time, dtype=jnp.float32)
    omegas = (jnp.arange(count_freq, dtype=jnp.float32) + 1.0) * (2.0 * math.pi / total_time)
    phase = omegas[:, None] * times[None, :]
    stacked = jnp.concatenate([jnp.cos(phase), -jnp.sin(phase)], 0)
    kept_times = (jnp.arange(total_time, dtype=jnp.int32) < onset).astype(jnp.float32)
    return jnp.dot(stacked * kept_times[None, :], (2.0 / total_time) * stacked.T, precision=lax.Precision.HIGHEST)


def apply_window(field, onsets):
    def single(block, onset):
        matrix = window_matrix(onset, F)
        result = jnp.dot(matrix, block.reshape(2 * F, -1), precision=lax.Precision.HIGHEST)
        return result.reshape(block.shape)
    return jax.vmap(single, in_axes=(2, 0), out_axes=2)(field, onsets)


def round_trip(values):
    return lax.optimization_barrier(values.astype(jnp.bfloat16)).astype(jnp.float32)


def slot_mask(rank_block):
    slots = jnp.arange(RMAX, dtype=jnp.int32)
    return (slots[None, None, :] < rank_block[:, :, None]).astype(jnp.float32)[..., None]


def forward_one(inputs):
    source_b, u_freq, v_freq, rank_block = inputs
    source32 = source_b.astype(jnp.float32)
    u32 = u_freq.astype(jnp.float32)
    v32 = v_freq.astype(jnp.float32)
    pattern = 'ijsn,jnp->ijsp'
    real_w = jnp.einsum(pattern, v32[0], source32[0]) - jnp.einsum(pattern, v32[1], source32[1])
    imag_w = jnp.einsum(pattern, v32[0], source32[1]) + jnp.einsum(pattern, v32[1], source32[0])
    masked = slot_mask(rank_block)
    real_w = round_trip(real_w * masked)
    imag_w = round_trip(imag_w * masked)
    pattern = 'ijsm,ijsp->imp'
    real_y = jnp.einsum(pattern, u32[0], real_w) - jnp.einsum(pattern, u32[1], imag_w)
    imag_y = jnp.einsum(pattern, u32[0], imag_w) + jnp.einsum(pattern, u32[1], real_w)
    return jnp.stack([real_y, imag_y], 0)


def adjoint_one(inputs):
    minus_b, u_freq, v_freq, rank_block = inputs
    minus32 = minus_b.astype(jnp.float32)
    u32 = u_freq.astype(jnp.float32)
    v32 = v_freq.astype(jnp.float32)
    pattern = 'ijsm,imp->ijsp'
    real_q = jnp.einsum(pattern, u32[0], minus32[0]) + jnp.einsum(pattern, u32[1], minus32[1])
    imag_q = jnp.einsum(pattern, u32[0], minus32[1]) - jnp.einsum(pattern, u32[1], minus32[0])
    masked = slot_mask(rank_block)
    real_q = round_trip(real_q * masked)
    imag_q = round_trip(imag_q * masked)
    pattern = 'ijsn,ijsp->jnp'
    real_p = jnp.einsum(pattern, v32[0], real_q) + jnp.einsum(pattern, v32[1], imag_q)
    imag_p = jnp.einsum(pattern, v32[0], imag_q) - jnp.einsum(pattern, v32[1], real_q)
    return jnp.stack([real_p, imag_p], 0)


def reference(start_field, u_tiles, v_tiles, ranks, onset_rec, onset_src):
    u_moved = jnp.moveaxis(u_tiles, 1, 0)
    v_moved = jnp.moveaxis(v_tiles, 1, 0)
    current = start_field
    minus_tiles = None
    for sweep_index in range(ITERS):
        source_b = current.astype(jnp.bfloat16).reshape(2, F, NTC, NBC, NP)
        image = lax.map(forward_one, (jnp.moveaxis(source_b, 1, 0), u_moved, v_moved, ranks))
        image = jnp.moveaxis(image, 0, 1)
        minus_tiles = apply_window(image, onset_rec)
        minus_b = minus_tiles.astype(jnp.bfloat16)
        back = lax.map(adjoint_one, (jnp.moveaxis(minus_b, 1, 0), u_moved, v_moved, ranks))
        back = jnp.moveaxis(back, 0, 1)
        current = start_field + apply_window(back, onset_src).reshape(2, F, NS, NP)
    return current, minus_tiles.reshape(2, F, NR, NP)
```

```python
import functools
import math

import jax
import jax.numpy as jnp
import numpy as np
from jax import lax
from jax.experimental import pallas as pl
from jax.experimental.pallas import tpu as pltpu
from jax.sharding import PartitionSpec as P

ITERS = 2
STEPS = 2 * ITERS
CHAINS = 2
NY, NX, NC = 4, 4, 2
NT = NY * NX * NC
NF = 8
GROUP = NX * NC
SLOTS = 64
GS = GROUP * SLOTS
POS = 512
POINTS = 128
ROWS = 2 * POINTS // CHAINS
CHUNK = ROWS // NF
PC = CHUNK // 2
TIMES = 4 * NF
MESH = pl.DeviceIdType.MESH
BF = jnp.bfloat16
F32 = jnp.float32
Y_ORDER = (2, 1, 3, 0)
X_ORDER = (2, 1, 3, 0)
Z_ORDER = (4, 3, 5, 2, 6, 1, 7)


def dot(a, b):
    return jnp.dot(a, b, preferred_element_type=F32)


def phase_rows():
    times = np.arange(TIMES, dtype=np.float64)
    omegas = (np.arange(NF, dtype=np.float64) + 1.0) * (2.0 * math.pi / TIMES)
    phase = omegas[:, None] * times[None, :]
    both = np.stack([np.cos(phase), -np.sin(phase)], 1)
    return np.repeat(both.reshape(2 * NF, TIMES), PC, axis=0).astype(np.float32)


def combine(first, second, sign):
    first = first.reshape(NF, 2, PC, first.shape[-1])
    second = second.reshape(NF, 2, PC, second.shape[-1]) * sign
    real = first[:, 0] - second[:, 1]
    imag = first[:, 1] + second[:, 0]
    return jnp.stack([real, imag], 1).reshape(ROWS, first.shape[-1])


def kernel(
    ranks, onset_rec, onset_src, phases, phases_t, start, u_hbm, v_hbm, plus_out, minus_out,
    nat, tr, st, w_send, w_recv, z1_send, z1_recv, z2_send, z2_recv, mask, window,
    load_sem, ws_sem, wr_sem, z1s_sem, z1r_sem, z2s_sem, z2r_sem,
):
    f = lax.axis_index("freq")
    me = lax.axis_index("tile")
    y, x, c = me // GROUP, (me // NC) % NX, me % NC

    def tile_of(dy, dx, dc):
        return ((y + dy) % NY) * GROUP + ((x + dx) % NX) * NC + (c + dc) % NC

    barrier = pltpu.get_barrier_semaphore()
    def load(which, group):
        source = v_hbm if which == 1 else u_hbm
        return pltpu.make_async_copy(source.at[:, group], nat.at[which, :, group], load_sem.at[which, group])

    for which in (1, 0):
        for group in range(NY):
            load(which, group).start()
    for dy in range(NY):
        for dx in range(NX):
            for dc in range(NC):
                if (dy, dx, dc) != (0, 0, 0):
                    pl.semaphore_signal(barrier, inc=1, device_id=(f, tile_of(dy, dx, dc)), device_id_type=MESH)
    for dz in range(1, NF):
        pl.semaphore_signal(barrier, inc=1, device_id=((f + dz) % NF, me), device_id_type=MESH)

    for part in range(2):
        turned = start[part].T
        for h in range(CHAINS):
            for k in range(NF):
                p0 = h * (POINTS // CHAINS) + k * PC
                r0 = k * CHUNK + part * PC
                st[h, r0 : r0 + PC, :] = turned[p0 : p0 + PC, :]
    for h in range(CHAINS):
        z2_recv[0, h] = jnp.zeros((NF, CHUNK, POS), BF)

    lanes = lax.broadcasted_iota(jnp.int32, (1, 2 * SLOTS), 1)
    for pair in range(NT // 2):
        group, l0 = pair // (GROUP // 2), pair % (GROUP // 2) * 2 * SLOTS
        for adj in range(2):
            low = ranks[2 * pair, me] if adj == 0 else ranks[me, 2 * pair]
            high = ranks[2 * pair + 1, me] if adj == 0 else ranks[me, 2 * pair + 1]
            bound = jnp.where(lanes < SLOTS, low, high + SLOTS)
            mask[adj, group, :, l0 : l0 + 2 * SLOTS] = jnp.where(lanes < bound, 1.0, 0.0).astype(F32)

    for group in range(NY):
        load(1, group).wait()
        for part in range(2):
            tr[0, part, group] = nat[1, part, group].T

    pl.semaphore_wait(barrier, NT - 1 + NF - 1)

    def setup_late():
        for adj, onset in ((0, onset_rec), (1, onset_src)):
            ticks = lax.broadcasted_iota(jnp.int32, (1, TIMES), 1)
            kept = jnp.where(ticks < onset[0], 1.0, 0.0).astype(F32)
            full = jnp.dot(phases[...] * kept, phases_t[...], precision=lax.Precision.HIGHEST, preferred_element_type=F32)
            r = lax.broadcasted_iota(jnp.int32, (ROWS, ROWS), 0)
            q = lax.broadcasted_iota(jnp.int32, (ROWS, ROWS), 1)
            full = jnp.where(r % PC == q % PC, full, 0.0)
            high = full.astype(BF)
            rest = full - high.astype(F32)
            middle = rest.astype(BF)
            low = (rest - middle.astype(F32)).astype(BF)
            window[adj, 0] = high
            window[adj, 1] = middle
            window[adj, 2] = low
        for group in range(NY):
            load(0, group).wait()
            for part in range(2):
                tr[1, part, group] = nat[0, part, group].T

    def coefficients(t, h, adj, sign):
        even = (1 - adj).astype(F32)

        @pl.when(t > 0)
        def _():
            z_wait(z2_recv.at[t, h], z2r_sem.at[t - 1, h])

        field = (st[h] * even + z2_recv[t, h].reshape(ROWS, POS).astype(F32)).astype(BF)
        for dy in Y_ORDER:
            group = (y + dy) % NY
            w = combine(dot(field, tr[adj, 0, group]), dot(field, tr[adj, 1, group]), sign)
            w = (w * mask[adj, group]).astype(BF)
            w_send[t, h, group] = w.T
            for dx in X_ORDER:
                for dc in (1, 0):
                    to = ((x + dx) % NX) * NC + (c + dc) % NC
                    chunk = w_send.at[t, h, group, pl.ds(to * SLOTS, SLOTS)]
                    mine = pl.ds((me % GROUP) * SLOTS, SLOTS)
                    if (dy, dx, dc) == (0, 0, 0):
                        w_recv[t, h, y, mine] = w_send[t, h, group, pl.ds(to * SLOTS, SLOTS)]
                        continue
                    pltpu.make_async_remote_copy(
                        src_ref=chunk, dst_ref=w_recv.at[t, h, y, mine],
                        send_sem=ws_sem.at[t, h], recv_sem=wr_sem.at[t, h, dy],
                        device_id=(f, group * GROUP + to), device_id_type=MESH,
                    ).start()

    def z_wait(buffer, semaphore):
        part = buffer.at[pl.ds(0, NF - 1)]
        pltpu.make_async_copy(part, part, semaphore).wait()

    def z_send(source, target, send_sem, recv_sem):
        for dz in Z_ORDER:
            to = (f + dz) % NF
            pltpu.make_async_remote_copy(
                src_ref=source.at[to], dst_ref=target.at[f], send_sem=send_sem, recv_sem=recv_sem,
                device_id=(to, me), device_id_type=MESH,
            ).start()

    def apply(t, h, adj, sign):
        real = imag = None
        for dy in Y_ORDER:
            group = (y - dy + NY) % NY
            count = GS - SLOTS if dy == 0 else GS
            part = w_recv.at[t, h, group, pl.ds(0, count)]
            pltpu.make_async_copy(part, part, wr_sem.at[t, h, dy]).wait()
            w = w_recv[t, h, group].T
            one, two = dot(w, nat[adj, 0, group]), dot(w, nat[adj, 1, group])
            real, imag = (one, two) if real is None else (real + one, imag + two)
        image = combine(real, imag, sign).astype(BF)
        z1_send[t, h] = image.reshape(NF, CHUNK, POS)
        z1_recv[t, h, f] = z1_send[t, h, f]
        z_send(z1_send.at[t, h], z1_recv.at[t, h], z1s_sem.at[t, h], z1r_sem.at[t, h])

    def windowed(t, h, adj):
        z_wait(z1_recv.at[t, h], z1r_sem.at[t, h])
        traces = z1_recv[t, h].reshape(ROWS, POS)
        out = dot(window[adj, 2], traces) + dot(window[adj, 1], traces) + dot(window[adj, 0], traces)
        z2_send[t, h] = out.astype(BF).reshape(NF, CHUNK, POS)
        z2_recv[t + 1, h, f] = z2_send[t, h, f]
        z_send(z2_send.at[t, h], z2_recv.at[t + 1, h], z2s_sem.at[t, h], z2r_sem.at[t, h])

    def turn_out(t, out, with_start):
        for part in range(2):
            rows = []
            for h in range(CHAINS):
                values = z2_recv[t, h].astype(F32).reshape(ROWS, POS)
                if with_start:
                    values = st[h] + values
                rows.append(values.reshape(NF, 2, PC, POS)[:, part].reshape(ROWS // 2, POS))
            out[part] = jnp.concatenate(rows, 0).T

    def body(t, carry):
        adj = t % 2
        sign = (1 - 2 * adj).astype(F32)
        for h in range(CHAINS):
            coefficients(t, h, adj, sign)
        pl.when(t == 0)(setup_late)
        pl.when(t == STEPS - 1)(lambda: turn_out(STEPS - 1, minus_out, False))
        for h in range(CHAINS):
            apply(t, h, adj, sign)
        for h in range(CHAINS):
            windowed(t, h, adj)
        return carry

    lax.fori_loop(0, STEPS, body, 0)
    for h in range(CHAINS):
        z_wait(z2_recv.at[STEPS, h], z2r_sem.at[STEPS - 1, h])
    turn_out(STEPS, plus_out, True)

    def drain(t, carry):
        for h in range(CHAINS):
            part = w_send.at[t, h, pl.ds(0, NY), pl.ds(0, GS)]
            for group in range(NY):
                count = GS - SLOTS if group == 0 else GS
                part = w_send.at[t, h, group, pl.ds(0, count)]
                pltpu.make_async_copy(part, part, ws_sem.at[t, h]).wait()
            z_wait(z1_send.at[t, h], z1s_sem.at[t, h])
            z_wait(z2_send.at[t, h], z2s_sem.at[t, h])
        return carry

    lax.fori_loop(0, STEPS, drain, 0)


def on_device(start_field, u_tiles, v_tiles, ranks, onset_rec, onset_src):
    rows = phase_rows()
    smem = pl.BlockSpec(memory_space=pltpu.SMEM)
    vmem = pl.BlockSpec(memory_space=pltpu.VMEM)
    hbm = pl.BlockSpec(memory_space=pl.ANY)
    field = jax.ShapeDtypeStruct((2, POS, POINTS), F32)
    plus, minus = pl.pallas_call(
        kernel,
        out_shape=(field, field),
        in_specs=[smem, smem, smem, vmem, vmem, vmem, hbm, hbm],
        out_specs=(vmem, vmem),
        scratch_shapes=[
            pltpu.VMEM((2, 2, NY, GS, POS), BF),
            pltpu.VMEM((2, 2, NY, POS, GS), BF),
            pltpu.VMEM((CHAINS, ROWS, POS), F32),
            pltpu.VMEM((STEPS, CHAINS, NY, GS, ROWS), BF),
            pltpu.VMEM((STEPS, CHAINS, NY, GS, ROWS), BF),
            pltpu.VMEM((STEPS, CHAINS, NF, CHUNK, POS), BF),
            pltpu.VMEM((STEPS, CHAINS, NF, CHUNK, POS), BF),
            pltpu.VMEM((STEPS, CHAINS, NF, CHUNK, POS), BF),
            pltpu.VMEM((STEPS + 1, CHAINS, NF, CHUNK, POS), BF),
            pltpu.VMEM((2, NY, 1, GS), F32),
            pltpu.VMEM((2, 3, ROWS, ROWS), BF),
            pltpu.SemaphoreType.DMA((2, NY)),
            pltpu.SemaphoreType.DMA((STEPS, CHAINS)),
            pltpu.SemaphoreType.DMA((STEPS, CHAINS, NY)),
            pltpu.SemaphoreType.DMA((STEPS, CHAINS)),
            pltpu.SemaphoreType.DMA((STEPS, CHAINS)),
            pltpu.SemaphoreType.DMA((STEPS, CHAINS)),
            pltpu.SemaphoreType.DMA((STEPS, CHAINS)),
        ],
        compiler_params=pltpu.CompilerParams(
            collective_id=0, has_side_effects=True, vmem_limit_bytes=52 * 2**20
        ),
        name="marchenko",
    )(
        ranks.reshape(NT, NT),
        onset_rec,
        onset_src,
        jnp.asarray(rows),
        jnp.asarray(2.0 / TIMES * rows.T),
        start_field.reshape(2, POS, POINTS),
        u_tiles.reshape(2, NY, GS, POS),
        v_tiles.reshape(2, NY, GS, POS),
    )
    shape = (2, 1, POS, POINTS)
    return plus.reshape(shape), minus.reshape(shape)


def solution(mesh):
    in_specs = (
        P(None, "freq", "tile", None),
        P(None, "freq", "tile", None, None, None),
        P(None, "freq", None, "tile", None, None),
        P("freq", None, None),
        P("tile"),
        P("tile"),
    )
    out_specs = (P(None, "freq", "tile", None), P(None, "freq", "tile", None))
    return jax.shard_map(
        on_device, mesh=mesh, in_specs=in_specs, out_specs=out_specs, check_vma=False
    )
```

```python
import functools
import math

import jax
import jax.numpy as jnp
import numpy as np
from jax import lax
from jax.experimental import pallas as pl
from jax.experimental.pallas import tpu as pltpu
from jax.sharding import PartitionSpec as P

ITERS = 2
STEPS = 2 * ITERS
CHAINS = 4
NY, NX, NC = 4, 4, 2
NT = NY * NX * NC
NF = 8
GROUP = NX * NC
SLOTS = 64
PACK = 2
PS = SLOTS // PACK
GP = GROUP * PS
GS = GROUP * SLOTS
POS = 512
POINTS = 128
PC = 8
ROWS = 2 * POINTS // CHAINS
CHUNK = 2 * PC
PCS = ROWS // CHUNK
CUTS = NF // PCS
WIDE = POS // CUTS
ALL = NF * CHUNK
TIMES = 4 * NF
MESH = pl.DeviceIdType.MESH
BF = jnp.bfloat16
F32 = jnp.float32
Y_ORDER = (2, 1, 3, 0)
X_ORDER = (2, 1, 3, 0)
Z_ORDER = (4, 3, 5, 2, 6, 1, 7)
ORDER = (
    ("S1", 0, 0), ("W", 2, 1), ("S1", 1, 0), ("W", 3, 1), ("U", 0, 0), ("S2", 0, 0), ("S1", 2, 0), ("C", 0, 0),
    ("S2", 1, 0), ("S1", 3, 0), ("UT", 0, 0), ("OUT", 0, 0), ("W", 0, 0), ("S2", 2, 0), ("W", 1, 0), ("S2", 3, 0),
)


def dot(a, b):
    return jnp.dot(a, b, preferred_element_type=F32)


def dot_nt(a, b):
    return lax.dot_general(a, b, (((1,), (1,)), ((), ())), preferred_element_type=F32)


def phase_rows():
    times = np.arange(TIMES, dtype=np.float64)
    omegas = (np.arange(NF, dtype=np.float64) + 1.0) * (2.0 * math.pi / TIMES)
    phase = omegas[:, None] * times[None, :]
    both = np.stack([np.cos(phase), -np.sin(phase)], 1)
    return np.repeat(both.reshape(2 * NF, TIMES), PC, axis=0).astype(np.float32)


def combine(first, second, sign):
    first = first.reshape(PCS, 2, PC, first.shape[-1])
    second = second.reshape(PCS, 2, PC, second.shape[-1]) * sign
    real = first[:, 0] - second[:, 1]
    imag = first[:, 1] + second[:, 0]
    return jnp.stack([real, imag], 1).reshape(ROWS, first.shape[-1])


def to_chunks(field):
    parts = [field[:, i * WIDE : (i + 1) * WIDE].reshape(PCS, CHUNK, WIDE) for i in range(CUTS)]
    return jnp.stack(parts, 1).reshape(NF, CHUNK, WIDE)


def from_chunks(chunks):
    chunks = chunks.reshape(PCS, CUTS, CHUNK, WIDE)
    return jnp.concatenate([chunks[:, i].reshape(ROWS, WIDE) for i in range(CUTS)], 1)


def kernel(
    onset_rec, onset_src, ranks_hbm, phases_hbm, phases_t_hbm, start_hbm, u_hbm, v_hbm, fields_out,
    nat, tr, start, st, w_send, w_recv, z1_send, z1_recv, z2_send, z2_recv, mask, window, phases, phases_t, ranks,
    small_sem, out_sem, load_sem, ws_sem, wr_sem, z1s_sem, z1r_sem, z2s_sem, z2r_sem,
):
    f = lax.axis_index("freq")
    me = lax.axis_index("tile")
    y, x, c = me // GROUP, (me // NC) % NX, me % NC

    def tile_of(dy, dx, dc):
        return ((y + dy) % NY) * GROUP + ((x + dx) % NX) * NC + (c + dc) % NC

    small = [
        pltpu.make_async_copy(source, target, small_sem.at[i])
        for i, (source, target) in enumerate(
            ((start_hbm, start), (ranks_hbm, ranks), (phases_hbm, phases), (phases_t_hbm, phases_t))
        )
    ]

    def load(which, group, part):
        source = (u_hbm, v_hbm)[which]
        slots = source.at[:, group, :, pl.ds(part * PS, PS)]
        return pltpu.make_async_copy(slots, nat.at[which, :, group, part], load_sem.at[which, group, part])

    def loads(which):
        return [load(which, (y + dy) % NY, part) for dy in Y_ORDER for part in range(PACK)]

    def tiles(which, part, group):
        return nat[which, part, group].reshape(GS, POS)

    small[0].start()
    small[1].start()
    for copy in loads(1):
        copy.start()
    barrier = pltpu.get_barrier_semaphore()
    for dy in range(NY):
        for dx in range(NX):
            for dc in range(NC):
                if (dy, dx, dc) != (0, 0, 0):
                    pl.semaphore_signal(barrier, inc=1, device_id=(f, tile_of(dy, dx, dc)), device_id_type=MESH)
    for dz in range(1, NF):
        pl.semaphore_signal(barrier, inc=1, device_id=((f + dz) % NF, me), device_id_type=MESH)
    small[2].start()
    small[3].start()
    small[0].wait()

    for part in range(2):
        turned = start[part].T.reshape(CHAINS, PCS, PC, POS)
        for h in range(CHAINS):
            for k in range(PCS):
                r0 = k * CHUNK + part * PC
                st[h, r0 : r0 + PC, :] = turned[h, k]
    for h in range(CHAINS):
        z2_recv[0, h] = jnp.zeros((NF, CHUNK, WIDE), BF)

    small[1].wait()
    lanes = lax.broadcasted_iota(jnp.int32, (1, 128), 1)
    across = 128 // PS
    for adj in range(2):
        for group in range(NY):
            for quad in range(GROUP // across):
                rank = None
                for i in range(across):
                    tile = group * GROUP + quad * across + i
                    one = ranks[tile, me] if adj == 0 else ranks[me, tile]
                    rank = one if rank is None else jnp.where(lanes < i * PS, rank, one)
                for part in range(PACK):
                    l0 = part * GP + quad * 128
                    slot = lanes % PS + part * PS
                    mask[adj, group, :, l0 : l0 + 128] = jnp.where(slot < rank, 1.0, 0.0).astype(F32)

    def wait_u():
        for copy in loads(0):
            copy.wait()

    def turn_u():
        for group in range(NY):
            for part in range(2):
                tr[1, part, group] = tiles(0, part, group).T

    def make_windows():
        small[2].wait()
        small[3].wait()
        for adj, onset in ((0, onset_rec), (1, onset_src)):
            ticks = lax.broadcasted_iota(jnp.int32, (1, TIMES), 1)
            kept = jnp.where(ticks < onset[0], 1.0, 0.0).astype(F32)
            full = jnp.dot(phases[...] * kept, phases_t[...], precision=lax.Precision.HIGHEST, preferred_element_type=F32)
            r = lax.broadcasted_iota(jnp.int32, (ALL, ALL), 0)
            q = lax.broadcasted_iota(jnp.int32, (ALL, ALL), 1)
            full = jnp.where(r % PC == q % PC, full, 0.0)
            high = full.astype(BF)
            rest = full - high.astype(F32)
            middle = rest.astype(BF)
            low = (rest - middle.astype(F32)).astype(BF)
            window[adj, 0] = high
            window[adj, 1] = middle
            window[adj, 2] = low

    def send_group(t, h, dy, w):
        group = (y + dy) % NY
        w = jnp.concatenate([w[:, i * GP : (i + 1) * GP] for i in range(PACK)], 0).T
        w_send[t, h, pl.ds(group * GP, GP)] = w
        for dx in X_ORDER:
            for dc in (1, 0):
                to = group * GROUP + ((x + dx) % NX) * NC + (c + dc) % NC
                theirs, mine = pl.ds(to * PS, PS), pl.ds(me * PS, PS)
                if (dy, dx, dc) == (0, 0, 0):
                    w_recv[t, h, mine] = w_send[t, h, mine]
                    continue
                pltpu.make_async_remote_copy(
                    src_ref=w_send.at[t, h, theirs], dst_ref=w_recv.at[t, h, mine],
                    send_sem=ws_sem.at[t, h], recv_sem=wr_sem.at[t, h, dy],
                    device_id=(f, to), device_id_type=MESH,
                ).start()

    def first_coefficients(h):
        field = st[h].astype(BF)
        for dy in Y_ORDER:
            group = (y + dy) % NY
            for part in range(PACK):
                load(1, group, part).wait()
            w = combine(dot_nt(field, tiles(1, 0, group)), dot_nt(field, tiles(1, 1, group)), 1.0)
            send_group(0, h, dy, (w * mask[0, group]).astype(BF))

    def coefficients(t, h):
        adj = t % 2
        sign = (1 - 2 * adj).astype(F32)
        even = (1 - adj).astype(F32)

        @pl.when(t > 0)
        def _():
            z_wait(z2_recv.at[t, h], z2r_sem.at[t - 1, h])

        field = (st[h] * even + from_chunks(z2_recv[t, h]).astype(F32)).astype(BF)
        for dy in Y_ORDER:
            group = (y + dy) % NY
            w = combine(dot(field, tr[adj, 0, group]), dot(field, tr[adj, 1, group]), sign)
            send_group(t, h, dy, (w * mask[adj, group]).astype(BF))

        @pl.when(t > 0)
        def _():
            drain(t - 1, h)

    def w_wait(buffer, semaphore, count):
        part = buffer.at[pl.ds(0, count * PS)]
        pltpu.make_async_copy(part, part, semaphore).wait()

    def z_wait(buffer, semaphore):
        part = buffer.at[pl.ds(0, NF - 1)]
        pltpu.make_async_copy(part, part, semaphore).wait()

    def drain(t, h):
        w_wait(w_send.at[t, h], ws_sem.at[t, h], NT - 1)
        z_wait(z1_send.at[t, h], z1s_sem.at[t, h])
        z_wait(z2_send.at[t, h], z2s_sem.at[t, h])

    def z_send(source, target, send_sem, recv_sem):
        for dz in Z_ORDER:
            to = (f + dz) % NF
            pltpu.make_async_remote_copy(
                src_ref=source.at[to], dst_ref=target.at[f], send_sem=send_sem, recv_sem=recv_sem,
                device_id=(to, me), device_id_type=MESH,
            ).start()

    def apply(t, h):
        adj = t % 2
        sign = (1 - 2 * adj).astype(F32)
        real = imag = None
        for dy in Y_ORDER:
            group = (y - dy + NY) % NY
            w_wait(w_recv.at[t, h], wr_sem.at[t, h, dy], GROUP - 1 if dy == 0 else GROUP)
            w = w_recv[t, h, pl.ds(group * GP, GP)].T
            w = jnp.concatenate([w[i * ROWS : (i + 1) * ROWS] for i in range(PACK)], 1)
            one, two = dot(w, tiles(adj, 0, group)), dot(w, tiles(adj, 1, group))
            real, imag = (one, two) if real is None else (real + one, imag + two)
        z1_send[t, h] = to_chunks(combine(real, imag, sign).astype(BF))
        z1_recv[t, h, f] = z1_send[t, h, f]
        z_send(z1_send.at[t, h], z1_recv.at[t, h], z1s_sem.at[t, h], z1r_sem.at[t, h])

    def windowed(t, h):
        adj = t % 2
        z_wait(z1_recv.at[t, h], z1r_sem.at[t, h])
        traces = z1_recv[t, h].reshape(ALL, WIDE)
        out = dot(window[adj, 2], traces) + dot(window[adj, 1], traces) + dot(window[adj, 0], traces)
        z2_send[t, h] = out.astype(BF).reshape(NF, CHUNK, WIDE)
        z2_recv[t + 1, h, f] = z2_send[t, h, f]
        z_send(z2_send.at[t, h], z2_recv.at[t + 1, h], z2s_sem.at[t, h], z2r_sem.at[t, h])

    def hand_out(which):
        return pltpu.make_async_copy(z2_recv.at[STEPS - 1 + which], fields_out.at[which], out_sem.at[which])

    pl.semaphore_wait(barrier, NT - 1 + NF - 1)
    first_coefficients(0)
    for copy in loads(0):
        copy.start()
    for group in range(NY):
        for part in range(2):
            tr[0, part, group] = tiles(1, part, group).T

    def body(t, carry):
        for stage, h, behind in ORDER:
            if stage == "S1" and h == 0:
                pl.when(t > 0)(lambda: coefficients(t, 0))
            elif stage == "S1":
                coefficients(t, h)
            elif stage == "S2":
                apply(t, h)
            elif stage == "W" and behind:
                pl.when(t > 0)(lambda h=h: windowed(t - 1, h))
            elif stage == "W":
                windowed(t, h)
            elif stage == "OUT":
                pl.when(t == STEPS - 1)(lambda: hand_out(0).start())
            else:
                pl.when(t == 0)({"U": wait_u, "C": make_windows, "UT": turn_u}[stage])
        return carry

    lax.fori_loop(0, STEPS, body, 0)
    for stage, h, behind in ORDER:
        if stage == "W" and behind:
            windowed(jnp.int32(STEPS - 1), h)
    for h in range(CHAINS):
        drain(STEPS - 1, h)
    for h in range(CHAINS):
        z_wait(z2_recv.at[STEPS, h], z2r_sem.at[STEPS - 1, h])
    hand_out(1).start()
    hand_out(0).wait()
    hand_out(1).wait()


def finish_kernel(start, fields, plus_out, minus_out):
    for part in range(2):
        for which, out in enumerate((minus_out, plus_out)):
            rows = [
                from_chunks(fields[which, h]).astype(F32).reshape(PCS, 2, PC, POS)[:, part].reshape(ROWS // 2, POS)
                for h in range(CHAINS)
            ]
            values = jnp.concatenate(rows, 0).T
            out[part] = start[part] + values if which else values


def on_device(start_field, u_tiles, v_tiles, ranks, onset_rec, onset_src):
    rows = phase_rows()
    smem = pl.BlockSpec(memory_space=pltpu.SMEM)
    vmem = pl.BlockSpec(memory_space=pltpu.VMEM)
    hbm = pl.BlockSpec(memory_space=pl.ANY)
    field = jax.ShapeDtypeStruct((2, POS, POINTS), F32)
    start_field = start_field.reshape(2, POS, POINTS)
    fields = pl.pallas_call(
        kernel,
        out_shape=jax.ShapeDtypeStruct((2, CHAINS, NF, CHUNK, WIDE), BF),
        in_specs=[smem, smem, hbm, hbm, hbm, hbm, hbm, hbm],
        out_specs=hbm,
        scratch_shapes=[
            pltpu.VMEM((2, 2, NY, PACK, GROUP, PS, POS), BF),
            pltpu.VMEM((2, 2, NY, POS, GS), BF),
            pltpu.VMEM((2, POS, POINTS), F32),
            pltpu.VMEM((CHAINS, ROWS, POS), F32),
            pltpu.VMEM((STEPS, CHAINS, NT * PS, PACK * ROWS), BF),
            pltpu.VMEM((STEPS, CHAINS, NT * PS, PACK * ROWS), BF),
            pltpu.VMEM((STEPS, CHAINS, NF, CHUNK, WIDE), BF),
            pltpu.VMEM((STEPS, CHAINS, NF, CHUNK, WIDE), BF),
            pltpu.VMEM((STEPS, CHAINS, NF, CHUNK, WIDE), BF),
            pltpu.VMEM((STEPS + 1, CHAINS, NF, CHUNK, WIDE), BF),
            pltpu.VMEM((2, NY, 1, GS), F32),
            pltpu.VMEM((2, 3, ALL, ALL), BF),
            pltpu.VMEM((ALL, TIMES), F32),
            pltpu.VMEM((TIMES, ALL), F32),
            pltpu.SMEM((NT, NT), jnp.int32),
            pltpu.SemaphoreType.DMA((4,)),
            pltpu.SemaphoreType.DMA((2,)),
            pltpu.SemaphoreType.DMA((2, NY, PACK)),
            pltpu.SemaphoreType.DMA((STEPS, CHAINS)),
            pltpu.SemaphoreType.DMA((STEPS, CHAINS, NY)),
            pltpu.SemaphoreType.DMA((STEPS, CHAINS)),
            pltpu.SemaphoreType.DMA((STEPS, CHAINS)),
            pltpu.SemaphoreType.DMA((STEPS, CHAINS)),
            pltpu.SemaphoreType.DMA((STEPS, CHAINS)),
        ],
        compiler_params=pltpu.CompilerParams(
            collective_id=0, has_side_effects=True, vmem_limit_bytes=63 * 2**20
        ),
        name="marchenko",
    )(
        onset_rec,
        onset_src,
        ranks.reshape(NT, NT),
        jnp.asarray(rows),
        jnp.asarray(2.0 / TIMES * rows.T),
        start_field,
        u_tiles.reshape(2, NY, GROUP, SLOTS, POS),
        v_tiles.reshape(2, NY, GROUP, SLOTS, POS),
    )
    plus, minus = pl.pallas_call(
        finish_kernel,
        out_shape=(field, field),
        in_specs=[vmem, vmem],
        out_specs=(vmem, vmem),
        name="finish",
    )(start_field, fields)
    shape = (2, 1, POS, POINTS)
    return plus.reshape(shape), minus.reshape(shape)


def solution(mesh):
    in_specs = (
        P(None, "freq", "tile", None),
        P(None, "freq", "tile", None, None, None),
        P(None, "freq", None, "tile", None, None),
        P("freq", None, None),
        P("tile"),
        P("tile"),
    )
    out_specs = (P(None, "freq", "tile", None), P(None, "freq", "tile", None))
    return jax.shard_map(
        on_device, mesh=mesh, in_specs=in_specs, out_specs=out_specs, check_vma=False
    )
```

```python
import functools
import math

import jax
import jax.numpy as jnp
import numpy as np
from jax import lax
from jax.experimental import pallas as pl
from jax.experimental.pallas import tpu as pltpu
from jax.sharding import PartitionSpec as P

ITERS = 2
STEPS = 2 * ITERS
CHAINS = 4
NY, NX, NC = 4, 4, 2
NT = NY * NX * NC
NF = 8
GROUP = NX * NC
SLOTS = 64
PACK = 2
PS = SLOTS // PACK
GP = GROUP * PS
GS = GROUP * SLOTS
POS = 512
POINTS = 128
PC = 8
ROWS = 2 * POINTS // CHAINS
CHUNK = 2 * PC
PCS = ROWS // CHUNK
CUTS = NF // PCS
WIDE = POS // CUTS
ALL = NF * CHUNK
TIMES = 4 * NF
MESH = pl.DeviceIdType.MESH
BF = jnp.bfloat16
F32 = jnp.float32
Y_ORDER = (2, 1, 3, 0)
X_ORDER = (2, 1, 3, 0)
Z_ORDER = (4, 3, 5, 2, 6, 1, 7)
ORDER = (
    ("S1", 0, 0), ("S2", 3, 1), ("W", 2, 1), ("S1", 1, 0), ("U", 0, 0), ("S2", 0, 0), ("W", 3, 1), ("C", 0, 0),
    ("S1", 2, 0), ("S2", 1, 0), ("UT", 0, 0), ("W", 0, 0), ("S1", 3, 0), ("OUT", 0, 0), ("S2", 2, 0), ("W", 1, 0),
)


def dot(a, b):
    return jnp.dot(a, b, preferred_element_type=F32)


def dot_nt(a, b):
    return lax.dot_general(a, b, (((1,), (1,)), ((), ())), preferred_element_type=F32)


def phase_rows():
    times = np.arange(TIMES, dtype=np.float64)
    omegas = (np.arange(NF, dtype=np.float64) + 1.0) * (2.0 * math.pi / TIMES)
    phase = omegas[:, None] * times[None, :]
    both = np.stack([np.cos(phase), -np.sin(phase)], 1)
    return np.repeat(both.reshape(2 * NF, TIMES), PC, axis=0).astype(np.float32)


def combine(first, second, sign):
    first = first.reshape(PCS, 2, PC, first.shape[-1])
    second = second.reshape(PCS, 2, PC, second.shape[-1]) * sign
    real = first[:, 0] - second[:, 1]
    imag = first[:, 1] + second[:, 0]
    return jnp.stack([real, imag], 1).reshape(ROWS, first.shape[-1])


def to_chunks(field):
    parts = [field[:, i * WIDE : (i + 1) * WIDE].reshape(PCS, CHUNK, WIDE) for i in range(CUTS)]
    return jnp.stack(parts, 1).reshape(NF, CHUNK, WIDE)


def from_chunks(chunks):
    chunks = chunks.reshape(PCS, CUTS, CHUNK, WIDE)
    return jnp.concatenate([chunks[:, i].reshape(ROWS, WIDE) for i in range(CUTS)], 1)


def kernel(
    onset_rec, onset_src, ranks_hbm, phases_hbm, phases_t_hbm, start_hbm, u_hbm, v_hbm, fields_out,
    nat, tr, start, st, w_send, w_recv, z1_send, z1_recv, z2_send, z2_recv, mask, window, phases, phases_t, ranks,
    small_sem, out_sem, load_sem, ws_sem, wr_sem, z1s_sem, z1r_sem, z2s_sem, z2r_sem,
):
    f = lax.axis_index("freq")
    me = lax.axis_index("tile")
    y, x, c = me // GROUP, (me // NC) % NX, me % NC

    def tile_of(dy, dx, dc):
        return ((y + dy) % NY) * GROUP + ((x + dx) % NX) * NC + (c + dc) % NC

    small = [
        pltpu.make_async_copy(source, target, small_sem.at[i])
        for i, (source, target) in enumerate(
            ((start_hbm, start), (ranks_hbm, ranks), (phases_hbm, phases), (phases_t_hbm, phases_t))
        )
    ]

    def load(which, group, part):
        source = (u_hbm, v_hbm)[which]
        slots = source.at[:, group, :, pl.ds(part * PS, PS)]
        return pltpu.make_async_copy(slots, nat.at[which, :, group, part], load_sem.at[which, group, part])

    def loads(which):
        return [load(which, (y + dy) % NY, part) for dy in Y_ORDER for part in range(PACK)]

    def tiles(which, part, group):
        return nat[which, part, group].reshape(GS, POS)

    small[0].start()
    small[1].start()
    for copy in loads(1):
        copy.start()
    barrier = pltpu.get_barrier_semaphore()
    for dy in range(NY):
        for dx in range(NX):
            for dc in range(NC):
                if (dy, dx, dc) != (0, 0, 0):
                    pl.semaphore_signal(barrier, inc=1, device_id=(f, tile_of(dy, dx, dc)), device_id_type=MESH)
    for dz in range(1, NF):
        pl.semaphore_signal(barrier, inc=1, device_id=((f + dz) % NF, me), device_id_type=MESH)
    small[2].start()
    small[3].start()
    small[0].wait()

    for part in range(2):
        turned = start[part].T.reshape(CHAINS, PCS, PC, POS)
        for h in range(CHAINS):
            for k in range(PCS):
                r0 = k * CHUNK + part * PC
                st[h, r0 : r0 + PC, :] = turned[h, k]
    for h in range(CHAINS):
        z2_recv[0, h] = jnp.zeros((NF, CHUNK, WIDE), BF)

    small[1].wait()
    lanes = lax.broadcasted_iota(jnp.int32, (1, 128), 1)
    across = 128 // PS
    for adj in range(2):
        for group in range(NY):
            for quad in range(GROUP // across):
                rank = None
                for i in range(across):
                    tile = group * GROUP + quad * across + i
                    one = ranks[tile, me] if adj == 0 else ranks[me, tile]
                    rank = one if rank is None else jnp.where(lanes < i * PS, rank, one)
                for part in range(PACK):
                    l0 = part * GP + quad * 128
                    slot = lanes % PS + part * PS
                    mask[adj, group, :, l0 : l0 + 128] = jnp.where(slot < rank, 1.0, 0.0).astype(F32)

    def wait_u():
        for copy in loads(0):
            copy.wait()

    def turn_u():
        for group in range(NY):
            for part in range(2):
                tr[1, part, group] = tiles(0, part, group).T

    def make_windows():
        small[2].wait()
        small[3].wait()
        for adj, onset in ((0, onset_rec), (1, onset_src)):
            ticks = lax.broadcasted_iota(jnp.int32, (1, TIMES), 1)
            kept = jnp.where(ticks < onset[0], 1.0, 0.0).astype(F32)
            full = jnp.dot(phases[...] * kept, phases_t[...], precision=lax.Precision.HIGHEST, preferred_element_type=F32)
            r = lax.broadcasted_iota(jnp.int32, (ALL, ALL), 0)
            q = lax.broadcasted_iota(jnp.int32, (ALL, ALL), 1)
            full = jnp.where(r % PC == q % PC, full, 0.0)
            high = full.astype(BF)
            rest = full - high.astype(F32)
            middle = rest.astype(BF)
            low = (rest - middle.astype(F32)).astype(BF)
            window[adj, 0] = high
            window[adj, 1] = middle
            window[adj, 2] = low

    def send_group(t, h, dy, w):
        group = (y + dy) % NY
        w = jnp.concatenate([w[:, i * GP : (i + 1) * GP] for i in range(PACK)], 0).T
        w_send[t, h, pl.ds(group * GP, GP)] = w
        for dx in X_ORDER:
            for dc in (1, 0):
                to = group * GROUP + ((x + dx) % NX) * NC + (c + dc) % NC
                theirs, mine = pl.ds(to * PS, PS), pl.ds(me * PS, PS)
                if (dy, dx, dc) == (0, 0, 0):
                    w_recv[t, h, mine] = w_send[t, h, mine]
                    continue
                pltpu.make_async_remote_copy(
                    src_ref=w_send.at[t, h, theirs], dst_ref=w_recv.at[t, h, mine],
                    send_sem=ws_sem.at[t, h], recv_sem=wr_sem.at[t, h, dy],
                    device_id=(f, to), device_id_type=MESH,
                ).start()

    def first_coefficients(h):
        field = st[h].astype(BF)
        for dy in Y_ORDER:
            group = (y + dy) % NY
            for part in range(PACK):
                load(1, group, part).wait()
            w = combine(dot_nt(field, tiles(1, 0, group)), dot_nt(field, tiles(1, 1, group)), 1.0)
            send_group(0, h, dy, (w * mask[0, group]).astype(BF))

    def coefficients(t, h):
        adj = t % 2
        sign = (1 - 2 * adj).astype(F32)
        even = (1 - adj).astype(F32)

        @pl.when(t > 0)
        def _():
            z_wait(z2_recv.at[t, h], z2r_sem.at[t - 1, h])

        field = (st[h] * even + from_chunks(z2_recv[t, h]).astype(F32)).astype(BF)
        for dy in Y_ORDER:
            group = (y + dy) % NY
            w = combine(dot(field, tr[adj, 0, group]), dot(field, tr[adj, 1, group]), sign)
            send_group(t, h, dy, (w * mask[adj, group]).astype(BF))

        @pl.when(t > 0)
        def _():
            drain(t - 1, h)

    def w_wait(buffer, semaphore, count):
        part = buffer.at[pl.ds(0, count * PS)]
        pltpu.make_async_copy(part, part, semaphore).wait()

    def z_wait(buffer, semaphore):
        part = buffer.at[pl.ds(0, NF - 1)]
        pltpu.make_async_copy(part, part, semaphore).wait()

    def drain(t, h):
        w_wait(w_send.at[t, h], ws_sem.at[t, h], NT - 1)
        z_wait(z1_send.at[t, h], z1s_sem.at[t, h])
        z_wait(z2_send.at[t, h], z2s_sem.at[t, h])

    def z_send(source, target, send_sem, recv_sem):
        for dz in Z_ORDER:
            to = (f + dz) % NF
            pltpu.make_async_remote_copy(
                src_ref=source.at[to], dst_ref=target.at[f], send_sem=send_sem, recv_sem=recv_sem,
                device_id=(to, me), device_id_type=MESH,
            ).start()

    def apply(t, h):
        adj = t % 2
        sign = (1 - 2 * adj).astype(F32)
        real = imag = None
        for dy in Y_ORDER:
            group = (y - dy + NY) % NY
            w_wait(w_recv.at[t, h], wr_sem.at[t, h, dy], GROUP - 1 if dy == 0 else GROUP)
            w = w_recv[t, h, pl.ds(group * GP, GP)].T
            w = jnp.concatenate([w[i * ROWS : (i + 1) * ROWS] for i in range(PACK)], 1)
            one, two = dot(w, tiles(adj, 0, group)), dot(w, tiles(adj, 1, group))
            real, imag = (one, two) if real is None else (real + one, imag + two)
        z1_send[t, h] = to_chunks(combine(real, imag, sign).astype(BF))
        z1_recv[t, h, f] = z1_send[t, h, f]
        z_send(z1_send.at[t, h], z1_recv.at[t, h], z1s_sem.at[t, h], z1r_sem.at[t, h])

    def windowed(t, h):
        adj = t % 2
        z_wait(z1_recv.at[t, h], z1r_sem.at[t, h])
        traces = z1_recv[t, h].reshape(ALL, WIDE)
        out = dot(window[adj, 2], traces) + dot(window[adj, 1], traces) + dot(window[adj, 0], traces)
        z2_send[t, h] = out.astype(BF).reshape(NF, CHUNK, WIDE)
        z2_recv[t + 1, h, f] = z2_send[t, h, f]
        z_send(z2_send.at[t, h], z2_recv.at[t + 1, h], z2s_sem.at[t, h], z2r_sem.at[t, h])

    def hand_out(which):
        return pltpu.make_async_copy(z2_recv.at[STEPS - 1 + which], fields_out.at[which], out_sem.at[which])

    pl.semaphore_wait(barrier, NT - 1 + NF - 1)
    first_coefficients(0)
    for copy in loads(0):
        copy.start()
    for group in range(NY):
        for part in range(2):
            tr[0, part, group] = tiles(1, part, group).T

    def body(t, carry):
        for stage, h, behind in ORDER:
            if stage == "S1" and h == 0:
                pl.when(t > 0)(lambda: coefficients(t, 0))
            elif stage == "S1":
                coefficients(t, h)
            elif stage == "S2" and behind:
                pl.when(t > 0)(lambda h=h: apply(t - 1, h))
            elif stage == "S2":
                apply(t, h)
            elif stage == "W" and behind:
                pl.when(t > 0)(lambda h=h: windowed(t - 1, h))
            elif stage == "W":
                windowed(t, h)
            elif stage == "OUT":
                pl.when(t == STEPS - 1)(lambda: hand_out(0).start())
            else:
                pl.when(t == 0)({"U": wait_u, "C": make_windows, "UT": turn_u}[stage])
        return carry

    lax.fori_loop(0, STEPS, body, 0)
    for stage, h, behind in ORDER:
        if behind:
            (apply if stage == "S2" else windowed)(jnp.int32(STEPS - 1), h)
    for h in range(CHAINS):
        drain(STEPS - 1, h)
    for h in range(CHAINS):
        z_wait(z2_recv.at[STEPS, h], z2r_sem.at[STEPS - 1, h])
    hand_out(1).start()
    hand_out(0).wait()
    hand_out(1).wait()


def finish_kernel(start, fields, plus_out, minus_out):
    for part in range(2):
        for which, out in enumerate((minus_out, plus_out)):
            rows = [
                fields[which, h].reshape(ROWS, WIDE).astype(F32).reshape(PCS, 2, PC, WIDE)[:, part].reshape(ROWS // 2, WIDE)
                for h in range(CHAINS)
            ]
            values = jnp.concatenate(rows, 0).T
            out[part] = start[part] + values if which else values


def on_device(start_field, u_tiles, v_tiles, ranks, onset_rec, onset_src):
    rows = phase_rows()
    smem = pl.BlockSpec(memory_space=pltpu.SMEM)
    vmem = pl.BlockSpec(memory_space=pltpu.VMEM)
    hbm = pl.BlockSpec(memory_space=pl.ANY)
    field = jax.ShapeDtypeStruct((2, POS, POINTS), F32)
    start_field = start_field.reshape(2, POS, POINTS)
    fields = pl.pallas_call(
        kernel,
        out_shape=jax.ShapeDtypeStruct((2, CHAINS, NF, CHUNK, WIDE), BF),
        in_specs=[smem, smem, hbm, hbm, hbm, hbm, hbm, hbm],
        out_specs=hbm,
        scratch_shapes=[
            pltpu.VMEM((2, 2, NY, PACK, GROUP, PS, POS), BF),
            pltpu.VMEM((2, 2, NY, POS, GS), BF),
            pltpu.VMEM((2, POS, POINTS), F32),
            pltpu.VMEM((CHAINS, ROWS, POS), F32),
            pltpu.VMEM((STEPS, CHAINS, NT * PS, PACK * ROWS), BF),
            pltpu.VMEM((STEPS, CHAINS, NT * PS, PACK * ROWS), BF),
            pltpu.VMEM((STEPS, CHAINS, NF, CHUNK, WIDE), BF),
            pltpu.VMEM((STEPS, CHAINS, NF, CHUNK, WIDE), BF),
            pltpu.VMEM((STEPS, CHAINS, NF, CHUNK, WIDE), BF),
            pltpu.VMEM((STEPS + 1, CHAINS, NF, CHUNK, WIDE), BF),
            pltpu.VMEM((2, NY, 1, GS), F32),
            pltpu.VMEM((2, 3, ALL, ALL), BF),
            pltpu.VMEM((ALL, TIMES), F32),
            pltpu.VMEM((TIMES, ALL), F32),
            pltpu.SMEM((NT, NT), jnp.int32),
            pltpu.SemaphoreType.DMA((4,)),
            pltpu.SemaphoreType.DMA((2,)),
            pltpu.SemaphoreType.DMA((2, NY, PACK)),
            pltpu.SemaphoreType.DMA((STEPS, CHAINS)),
            pltpu.SemaphoreType.DMA((STEPS, CHAINS, NY)),
            pltpu.SemaphoreType.DMA((STEPS, CHAINS)),
            pltpu.SemaphoreType.DMA((STEPS, CHAINS)),
            pltpu.SemaphoreType.DMA((STEPS, CHAINS)),
            pltpu.SemaphoreType.DMA((STEPS, CHAINS)),
        ],
        compiler_params=pltpu.CompilerParams(
            collective_id=0, has_side_effects=True, vmem_limit_bytes=63 * 2**20
        ),
        name="marchenko",
    )(
        onset_rec,
        onset_src,
        ranks.reshape(NT, NT),
        jnp.asarray(rows),
        jnp.asarray(2.0 / TIMES * rows.T),
        start_field,
        u_tiles.reshape(2, NY, GROUP, SLOTS, POS),
        v_tiles.reshape(2, NY, GROUP, SLOTS, POS),
    )
    cut = pl.BlockSpec((2, WIDE, POINTS), lambda i: (0, i, 0))
    plus, minus = pl.pallas_call(
        finish_kernel,
        out_shape=(field, field),
        grid=(CUTS,),
        in_specs=[cut, pl.BlockSpec((2, CHAINS, PCS, None, CHUNK, WIDE), lambda i: (0, 0, 0, i, 0, 0))],
        out_specs=(cut, cut),
        name="finish",
    )(start_field, fields.reshape(2, CHAINS, PCS, CUTS, CHUNK, WIDE))
    shape = (2, 1, POS, POINTS)
    return plus.reshape(shape), minus.reshape(shape)


def solution(mesh):
    in_specs = (
        P(None, "freq", "tile", None),
        P(None, "freq", "tile", None, None, None),
        P(None, "freq", None, "tile", None, None),
        P("freq", None, None),
        P("tile"),
        P("tile"),
    )
    out_specs = (P(None, "freq", "tile", None), P(None, "freq", "tile", None))
    return jax.shard_map(
        on_device, mesh=mesh, in_specs=in_specs, out_specs=out_specs, check_vma=False
    )
```

```python
import functools
import math

import jax
import jax.numpy as jnp
import numpy as np
from jax import lax
from jax.experimental import pallas as pl
from jax.experimental.pallas import tpu as pltpu
from jax.sharding import PartitionSpec as P

ITERS = 2
STEPS = 2 * ITERS
CHAINS = 4
NY, NX, NC = 4, 4, 2
NT = NY * NX * NC
NF = 8
GROUP = NX * NC
SLOTS = 64
PACK = 2
PS = SLOTS // PACK
GP = GROUP * PS
GS = GROUP * SLOTS
POS = 512
POINTS = 128
PC = 8
ROWS = 2 * POINTS // CHAINS
CHUNK = 2 * PC
PCS = ROWS // CHUNK
CUTS = NF // PCS
WIDE = POS // CUTS
ALL = NF * CHUNK
TIMES = 4 * NF
MESH = pl.DeviceIdType.MESH
BF = jnp.bfloat16
F32 = jnp.float32
Y_ORDER = (2, 1, 3, 0)
ARRIVAL = (0, 1, 3, 2)
X_ORDER = (2, 1, 3, 0)
Z_ORDER = (4, 3, 5, 2, 6, 1, 7)
ORDER = (
    ("S1", 0, 0), ("S2", 3, 1), ("W", 2, 1), ("S1", 1, 0), ("U", 0, 0), ("S2", 0, 0), ("W", 3, 1), ("C", 0, 0),
    ("S1", 2, 0), ("S2", 1, 0), ("UT", 0, 0), ("W", 0, 0), ("S1", 3, 0), ("OUT", 0, 0), ("S2", 2, 0), ("W", 1, 0),
)


def dot(a, b):
    return jnp.dot(a, b, preferred_element_type=F32)


def dot_nt(a, b):
    return lax.dot_general(a, b, (((1,), (1,)), ((), ())), preferred_element_type=F32)


def phase_rows():
    times = np.arange(TIMES, dtype=np.float64)
    omegas = (np.arange(NF, dtype=np.float64) + 1.0) * (2.0 * math.pi / TIMES)
    phase = omegas[:, None] * times[None, :]
    both = np.stack([np.cos(phase), -np.sin(phase)], 1)
    return np.repeat(both.reshape(2 * NF, TIMES), PC, axis=0).astype(np.float32)


def combine(first, second, sign):
    first = first.reshape(PCS, 2, PC, first.shape[-1])
    second = second.reshape(PCS, 2, PC, second.shape[-1]) * sign
    real = first[:, 0] - second[:, 1]
    imag = first[:, 1] + second[:, 0]
    return jnp.stack([real, imag], 1).reshape(ROWS, first.shape[-1])


def to_chunks(field):
    parts = [field[:, i * WIDE : (i + 1) * WIDE].reshape(PCS, CHUNK, WIDE) for i in range(CUTS)]
    return jnp.stack(parts, 1).reshape(NF, CHUNK, WIDE)


def from_chunks(chunks):
    chunks = chunks.reshape(PCS, CUTS, CHUNK, WIDE)
    return jnp.concatenate([chunks[:, i].reshape(ROWS, WIDE) for i in range(CUTS)], 1)


def kernel(
    onset_rec, onset_src, ranks_hbm, phases_hbm, phases_t_hbm, start_hbm, u_hbm, v_hbm, fields_out,
    nat, tr, start, st, w_send, w_recv, z1_send, z1_recv, z2_send, z2_recv, mask, window, phases, phases_t, ranks,
    small_sem, out_sem, load_sem, ws_sem, wr_sem, z1s_sem, z1r_sem, z2s_sem, z2r_sem,
):
    f = lax.axis_index("freq")
    me = lax.axis_index("tile")
    y, x, c = me // GROUP, (me // NC) % NX, me % NC

    def tile_of(dy, dx, dc):
        return ((y + dy) % NY) * GROUP + ((x + dx) % NX) * NC + (c + dc) % NC

    small = [
        pltpu.make_async_copy(source, target, small_sem.at[i])
        for i, (source, target) in enumerate(
            ((start_hbm, start), (ranks_hbm, ranks), (phases_hbm, phases), (phases_t_hbm, phases_t))
        )
    ]

    def load(which, group, part):
        source = (u_hbm, v_hbm)[which]
        slots = source.at[:, group, :, pl.ds(part * PS, PS)]
        return pltpu.make_async_copy(slots, nat.at[which, :, group, part], load_sem.at[which, group, part])

    def loads(which):
        return [load(which, (y + dy) % NY, part) for dy in Y_ORDER for part in range(PACK)]

    def tiles(which, part, group):
        return nat[which, part, group].reshape(GS, POS)

    small[0].start()
    small[1].start()
    for copy in loads(1):
        copy.start()
    barrier = pltpu.get_barrier_semaphore()
    for dy in range(NY):
        for dx in range(NX):
            for dc in range(NC):
                if (dy, dx, dc) != (0, 0, 0):
                    pl.semaphore_signal(barrier, inc=1, device_id=(f, tile_of(dy, dx, dc)), device_id_type=MESH)
    for dz in range(1, NF):
        pl.semaphore_signal(barrier, inc=1, device_id=((f + dz) % NF, me), device_id_type=MESH)
    small[2].start()
    small[3].start()
    small[0].wait()

    for part in range(2):
        turned = start[part].T.reshape(CHAINS, PCS, PC, POS)
        for h in range(CHAINS):
            for k in range(PCS):
                r0 = k * CHUNK + part * PC
                st[h, r0 : r0 + PC, :] = turned[h, k]
    for h in range(CHAINS):
        z2_recv[0, h] = jnp.zeros((NF, CHUNK, WIDE), BF)

    small[1].wait()
    lanes = lax.broadcasted_iota(jnp.int32, (1, 128), 1)
    across = 128 // PS
    for adj in range(2):
        for group in range(NY):
            for quad in range(GROUP // across):
                rank = None
                for i in range(across):
                    tile = group * GROUP + quad * across + i
                    one = ranks[tile, me] if adj == 0 else ranks[me, tile]
                    rank = one if rank is None else jnp.where(lanes < i * PS, rank, one)
                for part in range(PACK):
                    l0 = part * GP + quad * 128
                    slot = lanes % PS + part * PS
                    mask[adj, group, :, l0 : l0 + 128] = jnp.where(slot < rank, 1.0, 0.0).astype(F32)

    def wait_u():
        for copy in loads(0):
            copy.wait()

    def turn_u():
        for group in range(NY):
            for part in range(2):
                tr[1, part, group] = tiles(0, part, group).T

    def make_windows():
        small[2].wait()
        small[3].wait()
        for adj, onset in ((0, onset_rec), (1, onset_src)):
            ticks = lax.broadcasted_iota(jnp.int32, (1, TIMES), 1)
            kept = jnp.where(ticks < onset[0], 1.0, 0.0).astype(F32)
            full = jnp.dot(phases[...] * kept, phases_t[...], precision=lax.Precision.HIGHEST, preferred_element_type=F32)
            r = lax.broadcasted_iota(jnp.int32, (ALL, ALL), 0)
            q = lax.broadcasted_iota(jnp.int32, (ALL, ALL), 1)
            full = jnp.where(r % PC == q % PC, full, 0.0)
            high = full.astype(BF)
            rest = full - high.astype(F32)
            middle = rest.astype(BF)
            low = (rest - middle.astype(F32)).astype(BF)
            window[adj, 0] = high
            window[adj, 1] = middle
            window[adj, 2] = low

    def send_group(t, h, dy, w):
        group = (y + dy) % NY
        w = jnp.concatenate([w[:, i * GP : (i + 1) * GP] for i in range(PACK)], 0).T
        w_send[t, h, pl.ds(group * GP, GP)] = w
        for dx in X_ORDER:
            for dc in (1, 0):
                to = group * GROUP + ((x + dx) % NX) * NC + (c + dc) % NC
                theirs, mine = pl.ds(to * PS, PS), pl.ds(me * PS, PS)
                if (dy, dx, dc) == (0, 0, 0):
                    w_recv[t, h, mine] = w_send[t, h, mine]
                    continue
                pltpu.make_async_remote_copy(
                    src_ref=w_send.at[t, h, theirs], dst_ref=w_recv.at[t, h, mine],
                    send_sem=ws_sem.at[t, h], recv_sem=wr_sem.at[t, h, dy],
                    device_id=(f, to), device_id_type=MESH,
                ).start()

    def first_coefficients(h):
        field = st[h].astype(BF)
        for dy in Y_ORDER:
            group = (y + dy) % NY
            for part in range(PACK):
                load(1, group, part).wait()
            w = combine(dot_nt(field, tiles(1, 0, group)), dot_nt(field, tiles(1, 1, group)), 1.0)
            send_group(0, h, dy, (w * mask[0, group]).astype(BF))

    def coefficients(t, h):
        adj = t % 2
        sign = (1 - 2 * adj).astype(F32)
        even = (1 - adj).astype(F32)

        @pl.when(t > 0)
        def _():
            z_wait(z2_recv.at[t, h], z2r_sem.at[t - 1, h])

        field = (st[h] * even + from_chunks(z2_recv[t, h]).astype(F32)).astype(BF)
        for dy in Y_ORDER:
            group = (y + dy) % NY
            w = combine(dot(field, tr[adj, 0, group]), dot(field, tr[adj, 1, group]), sign)
            send_group(t, h, dy, (w * mask[adj, group]).astype(BF))

        @pl.when(t > 0)
        def _():
            drain(t - 1, h)

    def w_wait(buffer, semaphore, count):
        part = buffer.at[pl.ds(0, count * PS)]
        pltpu.make_async_copy(part, part, semaphore).wait()

    def z_wait(buffer, semaphore):
        part = buffer.at[pl.ds(0, NF - 1)]
        pltpu.make_async_copy(part, part, semaphore).wait()

    def drain(t, h):
        w_wait(w_send.at[t, h], ws_sem.at[t, h], NT - 1)
        z_wait(z1_send.at[t, h], z1s_sem.at[t, h])
        z_wait(z2_send.at[t, h], z2s_sem.at[t, h])

    def z_send(source, target, send_sem, recv_sem):
        for dz in Z_ORDER:
            to = (f + dz) % NF
            pltpu.make_async_remote_copy(
                src_ref=source.at[to], dst_ref=target.at[f], send_sem=send_sem, recv_sem=recv_sem,
                device_id=(to, me), device_id_type=MESH,
            ).start()

    def apply(t, h):
        adj = t % 2
        sign = (1 - 2 * adj).astype(F32)
        real = imag = None
        for dy in ARRIVAL:
            group = (y - dy + NY) % NY
            w_wait(w_recv.at[t, h], wr_sem.at[t, h, dy], GROUP - 1 if dy == 0 else GROUP)
            w = w_recv[t, h, pl.ds(group * GP, GP)].T
            w = jnp.concatenate([w[i * ROWS : (i + 1) * ROWS] for i in range(PACK)], 1)
            one, two = dot(w, tiles(adj, 0, group)), dot(w, tiles(adj, 1, group))
            real, imag = (one, two) if real is None else (real + one, imag + two)
        z1_send[t, h] = to_chunks(combine(real, imag, sign).astype(BF))
        z1_recv[t, h, f] = z1_send[t, h, f]
        z_send(z1_send.at[t, h], z1_recv.at[t, h], z1s_sem.at[t, h], z1r_sem.at[t, h])

    def windowed(t, h):
        adj = t % 2
        z_wait(z1_recv.at[t, h], z1r_sem.at[t, h])
        traces = z1_recv[t, h].reshape(ALL, WIDE)
        out = dot(window[adj, 2], traces) + dot(window[adj, 1], traces) + dot(window[adj, 0], traces)
        z2_send[t, h] = out.astype(BF).reshape(NF, CHUNK, WIDE)
        z2_recv[t + 1, h, f] = z2_send[t, h, f]
        z_send(z2_send.at[t, h], z2_recv.at[t + 1, h], z2s_sem.at[t, h], z2r_sem.at[t, h])

    def hand_out(which, h):
        source, target = z2_recv.at[STEPS - 1 + which, h], fields_out.at[which, h]
        return pltpu.make_async_copy(source, target, out_sem.at[which, h])

    def hand_out_first():
        for h in range(CHAINS):
            hand_out(0, h).start()

    pl.semaphore_wait(barrier, NT - 1 + NF - 1)
    first_coefficients(0)
    for copy in loads(0):
        copy.start()
    for group in range(NY):
        for part in range(2):
            tr[0, part, group] = tiles(1, part, group).T

    def body(t, carry):
        for stage, h, behind in ORDER:
            if stage == "S1" and h == 0:
                pl.when(t > 0)(lambda: coefficients(t, 0))
            elif stage == "S1":
                coefficients(t, h)
            elif stage == "S2" and behind:
                pl.when(t > 0)(lambda h=h: apply(t - 1, h))
            elif stage == "S2":
                apply(t, h)
            elif stage == "W" and behind:
                pl.when(t > 0)(lambda h=h: windowed(t - 1, h))
            elif stage == "W":
                windowed(t, h)
            elif stage == "OUT":
                pl.when(t == STEPS - 1)(hand_out_first)
            else:
                pl.when(t == 0)({"U": wait_u, "C": make_windows, "UT": turn_u}[stage])
        return carry

    lax.fori_loop(0, STEPS, body, 0)
    for stage, h, behind in ORDER:
        if behind:
            (apply if stage == "S2" else windowed)(jnp.int32(STEPS - 1), h)
    for h in range(CHAINS):
        drain(STEPS - 1, h)
    for h in range(CHAINS):
        z_wait(z2_recv.at[STEPS, h], z2r_sem.at[STEPS - 1, h])
        hand_out(1, h).start()
    for which in range(2):
        for h in range(CHAINS):
            hand_out(which, h).wait()


def finish_kernel(start, fields, plus_out, minus_out):
    for part in range(2):
        for which, out in enumerate((minus_out, plus_out)):
            rows = [
                fields[which, h].reshape(ROWS, WIDE).astype(F32).reshape(PCS, 2, PC, WIDE)[:, part].reshape(ROWS // 2, WIDE)
                for h in range(CHAINS)
            ]
            values = jnp.concatenate(rows, 0).T
            out[part] = start[part] + values if which else values


def on_device(start_field, u_tiles, v_tiles, ranks, onset_rec, onset_src):
    rows = phase_rows()
    smem = pl.BlockSpec(memory_space=pltpu.SMEM)
    vmem = pl.BlockSpec(memory_space=pltpu.VMEM)
    hbm = pl.BlockSpec(memory_space=pl.ANY)
    field = jax.ShapeDtypeStruct((2, POS, POINTS), F32)
    start_field = start_field.reshape(2, POS, POINTS)
    fields = pl.pallas_call(
        kernel,
        out_shape=jax.ShapeDtypeStruct((2, CHAINS, NF, CHUNK, WIDE), BF),
        in_specs=[smem, smem, hbm, hbm, hbm, hbm, hbm, hbm],
        out_specs=hbm,
        scratch_shapes=[
            pltpu.VMEM((2, 2, NY, PACK, GROUP, PS, POS), BF),
            pltpu.VMEM((2, 2, NY, POS, GS), BF),
            pltpu.VMEM((2, POS, POINTS), F32),
            pltpu.VMEM((CHAINS, ROWS, POS), F32),
            pltpu.VMEM((STEPS, CHAINS, NT * PS, PACK * ROWS), BF),
            pltpu.VMEM((STEPS, CHAINS, NT * PS, PACK * ROWS), BF),
            pltpu.VMEM((STEPS, CHAINS, NF, CHUNK, WIDE), BF),
            pltpu.VMEM((STEPS, CHAINS, NF, CHUNK, WIDE), BF),
            pltpu.VMEM((STEPS, CHAINS, NF, CHUNK, WIDE), BF),
            pltpu.VMEM((STEPS + 1, CHAINS, NF, CHUNK, WIDE), BF),
            pltpu.VMEM((2, NY, 1, GS), F32),
            pltpu.VMEM((2, 3, ALL, ALL), BF),
            pltpu.VMEM((ALL, TIMES), F32),
            pltpu.VMEM((TIMES, ALL), F32),
            pltpu.SMEM((NT, NT), jnp.int32),
            pltpu.SemaphoreType.DMA((4,)),
            pltpu.SemaphoreType.DMA((2, CHAINS)),
            pltpu.SemaphoreType.DMA((2, NY, PACK)),
            pltpu.SemaphoreType.DMA((STEPS, CHAINS)),
            pltpu.SemaphoreType.DMA((STEPS, CHAINS, NY)),
            pltpu.SemaphoreType.DMA((STEPS, CHAINS)),
            pltpu.SemaphoreType.DMA((STEPS, CHAINS)),
            pltpu.SemaphoreType.DMA((STEPS, CHAINS)),
            pltpu.SemaphoreType.DMA((STEPS, CHAINS)),
        ],
        compiler_params=pltpu.CompilerParams(
            collective_id=0, has_side_effects=True, vmem_limit_bytes=63 * 2**20
        ),
        name="marchenko",
    )(
        onset_rec,
        onset_src,
        ranks.reshape(NT, NT),
        jnp.asarray(rows),
        jnp.asarray(2.0 / TIMES * rows.T),
        start_field,
        u_tiles.reshape(2, NY, GROUP, SLOTS, POS),
        v_tiles.reshape(2, NY, GROUP, SLOTS, POS),
    )
    cut = pl.BlockSpec((2, WIDE, POINTS), lambda i: (0, i, 0))
    plus, minus = pl.pallas_call(
        finish_kernel,
        out_shape=(field, field),
        grid=(CUTS,),
        in_specs=[cut, pl.BlockSpec((2, CHAINS, PCS, None, CHUNK, WIDE), lambda i: (0, 0, 0, i, 0, 0))],
        out_specs=(cut, cut),
        name="finish",
    )(start_field, fields.reshape(2, CHAINS, PCS, CUTS, CHUNK, WIDE))
    shape = (2, 1, POS, POINTS)
    return plus.reshape(shape), minus.reshape(shape)


def solution(mesh):
    in_specs = (
        P(None, "freq", "tile", None),
        P(None, "freq", "tile", None, None, None),
        P(None, "freq", None, "tile", None, None),
        P("freq", None, None),
        P("tile"),
        P("tile"),
    )
    out_specs = (P(None, "freq", "tile", None), P(None, "freq", "tile", None))
    return jax.shard_map(
        on_device, mesh=mesh, in_specs=in_specs, out_specs=out_specs, check_vma=False
    )
```
